32 devices in a mesh: groups: 2 (over x), space: 16 (over z, y, core).
Axes of the slice: x: 2, y: 2, z: 4, core: 2. Of those that a mesh axis runs over, the one named last changes fastest.
Arguments:
- params: float32 [59, 262144], P(None, ('groups', 'space')), parts along dimension 1, may hold values from -6 to 3.2, as said below
- adam_m: float32 [59, 262144], P(None, ('groups', 'space')), parts along dimension 1, may hold values from -0.225 to 0.225
- adam_v: float32 [59, 262144], P(None, ('groups', 'space')), parts along dimension 1, may hold values from 5e-07 to 0.00045, as said below
- camera: float32 [12], P('groups'), parts along dimension 0, may hold values from -0.2 to 0.2
- target: float32 [256, 3, 256], P(('groups', 'space')), parts along dimension 0, may hold values from 0 to 1
- tile_ids: int32 [256], P(('groups', 'space')), parts along dimension 0, may hold values from 0 to 127, as said below
- tile_blocks: int32 [256], P(('groups', 'space')), parts along dimension 0, may hold values from 1 to 4, as said below
- tile_lists: int32 [256, 1024], P(('groups', 'space')), parts along dimension 0, may hold values from 0 to 8191, as said below
- send_rows: int32 [32, 16, 512], P(('groups', 'space')), parts along dimension 0, may hold values from 0 to 8191, as said below
Outputs:
- new_params: float32 [59, 262144], P(None, ('groups', 'space')), parts along dimension 1
- new_m: float32 [59, 262144], P(None, ('groups', 'space')), parts along dimension 1
- new_v: float32 [59, 262144], P(None, ('groups', 'space')), parts along dimension 1
The draws below stay inside these ranges and needn't reach their ends.
There are 2 independent parts, one for each index of `groups`. The reference program is written for one: setup_inputs(seed, part) draws one part's arguments, and reference() takes and returns one part's arrays. A program takes and returns all parts, laid end to end along the dimension named above; each array names one. Nothing has to cross between parts.
Inputs may be any that keep to these rules, and one draw needn't show every extreme that they name: send_rows[s, d] names 512 distinct local columns of owner s, in the order in which renderer d receives them; no column of an owner goes to two renderers. `tile_ids`: a permutation of the 128 image tiles. `tile_blocks`: each tile slot lists 256 times this many Gaussians; one renderer, drawn from the seed, has all its tile slots at 4. `tile_lists`: each row holds distinct indices into the renderer's received columns; its first 256 times tile_blocks entries are live and ordered by increasing camera depth p_z, nearest Gaussian first; no received column is live in two tile slots of one renderer; entries at or after 256 times tile_blocks are ignored. `params`: attribute ranges: the position (attributes 0 to 2) lies within distance 3.2 of the anchor, log scale log 0.01 to log 0.06, rotation entries -1 to 1 with the first raised by 1.5, opacity logit -6 to -2.5, harmonics -0.9 to 0.9. `adam_v`: positive.
All inputs are finite; a program needn't handle non-finite values.
Results may differ from the reference program's by a relative error of at most 0.0003.
Values sent between devices are 32-bit elements; how exact they have to be, the bound alone decides.
A program may use at most 128 MiB of HBM per device.

```python
import math
import jax
import jax.numpy as jnp
from jax import lax

G_DEV = 8192
RECV = 8192
TILE_DEV = 8
TILE_PIX = 256
BLOCK = 256
MAXBLK = 4
ADAM_STEP = 10
TILES = 128
LIST = 1024
CAP = 512
N_SPACE = 16


def view_angles(key):
    return jax.random.uniform(jax.random.fold_in(key, 101), (6,), jnp.float32, -0.2, 0.2)


def tile_order(key):
    return jax.random.permutation(jax.random.fold_in(key, 201), TILE_DEV * N_SPACE).astype(jnp.int32)


def tile_counts(key):
    tiles_all = TILE_DEV * N_SPACE
    heavy = jax.random.randint(jax.random.fold_in(key, 202), (tiles_all,), 0, 4) == 0
    lighter = jax.random.randint(jax.random.fold_in(key, 203), (tiles_all,), 1, MAXBLK)
    busiest = jax.random.randint(jax.random.fold_in(key, 204), (), 0, N_SPACE)
    renderer = jnp.arange(tiles_all, dtype=jnp.int32) // TILE_DEV
    return jnp.where(heavy | (renderer == busiest), MAXBLK, lighter).astype(jnp.int32)


def received_permutation(subkey):
    return jax.random.permutation(subkey, RECV).astype(jnp.int32)


def owner_permutation(subkey):
    return jax.random.permutation(subkey, G_DEV).astype(jnp.int32)


def received_orders(key):
    subkeys = jax.random.split(jax.random.fold_in(key, 205), N_SPACE)
    return jax.vmap(received_permutation)(subkeys)


def owner_orders(key):
    subkeys = jax.random.split(jax.random.fold_in(key, 206), N_SPACE)
    return jax.vmap(owner_permutation)(subkeys)


def slot_starts(blocks):
    slot_blocks = blocks.reshape(N_SPACE, TILE_DEV)
    starts = (jnp.cumsum(slot_blocks, axis=1) - slot_blocks) * BLOCK
    return (slot_blocks, starts)


def world_matrix(camera):
    cos_a, sin_a = (jnp.cos(camera[0]), jnp.sin(camera[0]))
    cos_b, sin_b = (jnp.cos(camera[1]), jnp.sin(camera[1]))
    cos_c, sin_c = (jnp.cos(camera[2]), jnp.sin(camera[2]))
    return [[cos_c * cos_b, cos_c * sin_b * sin_a - sin_c * cos_a, cos_c * sin_b * cos_a + sin_c * sin_a], [sin_c * cos_b, sin_c * sin_b * sin_a + cos_c * cos_a, sin_c * sin_b * cos_a - cos_c * sin_a], [-sin_b, cos_b * sin_a, cos_b * cos_a]]


def group_scale():
    return jnp.concatenate([jnp.full((3,), 0.15, jnp.float32), jnp.full((3,), 0.03, jnp.float32), jnp.full((4,), 0.01, jnp.float32), jnp.full((1,), 0.015, jnp.float32), jnp.full((3,), 0.03, jnp.float32), jnp.full((45,), 0.015, jnp.float32)])


def draw_camera(key, part):
    camera = view_angles(key)
    return camera


def draw_tile_ids(key, part):
    order = tile_order(key)
    return order


def draw_tile_blocks(key, part):
    blocks = tile_counts(key)
    return blocks


def draw_tile_lists(key, part):
    blocks = tile_counts(key)
    received = received_orders(key)
    slot_blocks, starts = slot_starts(blocks)
    places = (starts[:, :, None] + jnp.arange(LIST, dtype=jnp.int32)[None, None, :]) % RECV
    renderer = jnp.arange(N_SPACE, dtype=jnp.int32)[:, None, None]
    picked = received.reshape(-1)[renderer * RECV + places]
    return picked.reshape(TILE_DEV * N_SPACE, LIST).astype(jnp.int32)


def draw_send_rows(key, part):
    owners = owner_orders(key)
    return owners[:, :RECV].reshape(N_SPACE, N_SPACE, CAP).astype(jnp.int32)


def draw_params(key, part):
    camera = view_angles(key)
    order = tile_order(key)
    blocks = tile_counts(key)
    received = received_orders(key)
    owners = owner_orders(key)
    key = jax.random.fold_in(key, 17)
    subkeys = jax.random.split(key, 10)
    count = G_DEV * N_SPACE
    tiles_all = TILE_DEV * N_SPACE
    slot_blocks, starts = slot_starts(blocks)
    ends = starts + slot_blocks * BLOCK
    places = jnp.arange(RECV, dtype=jnp.int32)[None, :, None]
    inside = ((places >= starts[:, None, :]) & (places < ends[:, None, :])).astype(jnp.int32)
    live = jnp.sum(inside, axis=2)
    start_here = jnp.sum(inside * starts[:, None, :], axis=2)
    length_here = jnp.sum(inside * (slot_blocks * BLOCK)[:, None, :], axis=2)
    tile_here = jnp.sum(inside * order.reshape(N_SPACE, TILE_DEV)[:, None, :], axis=2)
    rank_here = (jnp.arange(RECV, dtype=jnp.int32)[None, :] - start_here) * live
    source = received // CAP
    within = received % CAP
    renderer = jnp.arange(N_SPACE, dtype=jnp.int32)[:, None]
    local = owners.reshape(-1)[source * G_DEV + renderer * CAP + within]
    column = (source * G_DEV + local).reshape(-1)
    live_col = jnp.zeros((count,), jnp.int32).at[column].set(live.reshape(-1))
    tile_col = jnp.zeros((count,), jnp.int32).at[column].set(tile_here.reshape(-1))
    rank_col = jnp.zeros((count,), jnp.int32).at[column].set(rank_here.reshape(-1))
    length_col = jnp.ones((count,), jnp.int32).at[column].set(jnp.maximum(length_here, 1).reshape(-1))
    focal_len = max(256, tiles_all) * 5.0 / 3.0
    center_y = tiles_all * 0.5
    jitter_x = jax.random.uniform(subkeys[0], (count,), jnp.float32, -2.0, 18.0)
    jitter_y = jax.random.uniform(subkeys[1], (count,), jnp.float32, -2.0, 18.0)
    wobble = jax.random.uniform(subkeys[2], (count,), jnp.float32)
    free_u = jax.random.uniform(subkeys[3], (count,), jnp.float32, 0.0, 256.0)
    free_v = jax.random.uniform(subkeys[4], (count,), jnp.float32, 0.0, tiles_all * 1.0)
    free_z = jax.random.uniform(subkeys[5], (count,), jnp.float32, 4.0, 6.0)
    drawn = live_col > 0
    screen_u = jnp.where(drawn, (16 * (tile_col % 16)).astype(jnp.float32) + jitter_x, free_u)
    screen_v = jnp.where(drawn, (16 * (tile_col // 16)).astype(jnp.float32) + jitter_y, free_v)
    depth_list = 4.0 + 2.0 * (rank_col.astype(jnp.float32) + 0.5 + 0.8 * (wobble - 0.5)) / length_col.astype(jnp.float32)
    depth = jnp.where(drawn, depth_list, free_z)
    world = world_matrix(camera)
    rel_x = (screen_u - 128.0) * depth / focal_len - camera[3]
    rel_y = (screen_v - center_y) * depth / focal_len - camera[4]
    rel_z = depth - (5.0 + camera[5])
    means = jnp.stack([world[0][axis_i] * rel_x + world[1][axis_i] * rel_y + world[2][axis_i] * rel_z for axis_i in range(3)])
    lowest, highest = (math.log(0.01), math.log(0.06))
    quaternion = jax.random.uniform(subkeys[7], (4, count), jnp.float32, -1.0, 1.0)
    quaternion = quaternion + jnp.array([1.5, 0.0, 0.0, 0.0], jnp.float32)[:, None]
    log_scales = jax.random.uniform(subkeys[6], (3, count), jnp.float32, lowest, highest)
    opacity = jax.random.uniform(subkeys[8], (1, count), jnp.float32, -6.0, -2.5)
    harmonics = 0.3 * jax.random.truncated_normal(subkeys[9], -3.0, 3.0, (48, count), jnp.float32)
    return jnp.concatenate([means, log_scales, quaternion, opacity, harmonics], axis=0)


def draw_adam_m(key, part):
    key = jax.random.fold_in(key, 41)
    count = G_DEV * N_SPACE
    scale = group_scale()[:, None]
    base = jax.random.truncated_normal(key, -3.0, 3.0, (59, count), jnp.float32)
    return 0.5 * scale * base


def draw_adam_v(key, part):
    key = jax.random.fold_in(key, 43)
    count = G_DEV * N_SPACE
    scale = group_scale()[:, None]
    factor = jnp.exp(jax.random.uniform(key, (59, count), jnp.float32, math.log(0.5), math.log(2.0)))
    return 0.01 * scale * scale * factor


def block_scale(key, dims, cuts, smallest, high):
    level = 1.0
    for dim, parts in cuts:
        heights = jax.random.uniform(jax.random.fold_in(jax.random.fold_in(key, 6), dim), (parts,), jnp.float32, smallest / len(cuts), high / len(cuts))
        level = level * jnp.repeat(jnp.exp(heights), dims[dim] // parts).reshape((-1,) + (1,) * (len(dims) - 1 - dim))
    return level


def setup_inputs(seed: int = 0, part: int = 0) -> dict:
    key_of = jax.random.split(jax.random.key(seed), 10)
    part_splits = jax.random.split(jax.random.fold_in(key_of[9], part), 10)
    params = draw_params(jax.random.fold_in(jax.random.fold_in(key_of[9], part), 71), part)
    adam_m = draw_adam_m(jax.random.fold_in(jax.random.fold_in(key_of[9], part), 71), part)
    adam_v = draw_adam_v(jax.random.fold_in(jax.random.fold_in(key_of[9], part), 71), part)
    camera = draw_camera(jax.random.fold_in(jax.random.fold_in(key_of[9], part), 71), part)
    target = jnp.clip(1.0 * jax.random.uniform(part_splits[4], (TILES, 3, TILE_PIX), jnp.float32) ** block_scale(part_splits[4], (TILES, 3, TILE_PIX), ((0, 16),), -0.2, 0.2), 0.0, 1.0)
    tile_ids = draw_tile_ids(jax.random.fold_in(jax.random.fold_in(key_of[9], part), 71), part)
    tile_blocks = draw_tile_blocks(jax.random.fold_in(jax.random.fold_in(key_of[9], part), 71), part)
    tile_lists = draw_tile_lists(jax.random.fold_in(jax.random.fold_in(key_of[9], part), 71), part)
    send_rows = draw_send_rows(jax.random.fold_in(jax.random.fold_in(key_of[9], part), 71), part)
    return {"params": params, "adam_m": adam_m, "adam_v": adam_v, "camera": camera, "target": target, "tile_ids": tile_ids, "tile_blocks": tile_blocks, "tile_lists": tile_lists, "send_rows": send_rows}


HIGHEST_PREC = lax.Precision.HIGHEST
BETA_ONE = 0.9
BETA_TWO = 0.999
ADAM_EPSILON = 1e-15
HARM_ZERO = 0.28209479177387814
HARM_ONE = 0.4886025119029199
HARM_TWO = (1.0925484305920792, -1.0925484305920792, 0.31539156525252005, -1.0925484305920792, 0.5462742152960396)
HARM_THREE = (-0.5900435899266435, 2.890611442640554, -0.4570457994644658, 0.3731763325901154, -0.4570457994644658, 1.445305721320277, -0.5900435899266435)

def geometry(tiles_all):
    focal_len = max(256, tiles_all) * 5.0 / 3.0
    center_y = tiles_all * 0.5
    return (focal_len, center_y)

def rotation_of(camera):
    one_val = jnp.ones_like(camera[0])
    zero_val = jnp.zeros_like(camera[0])
    cos_a, sin_a = (jnp.cos(camera[0]), jnp.sin(camera[0]))
    cos_b, sin_b = (jnp.cos(camera[1]), jnp.sin(camera[1]))
    cos_c, sin_c = (jnp.cos(camera[2]), jnp.sin(camera[2]))
    around_x = jnp.stack([jnp.stack([one_val, zero_val, zero_val]), jnp.stack([zero_val, cos_a, -sin_a]), jnp.stack([zero_val, sin_a, cos_a])])
    around_y = jnp.stack([jnp.stack([cos_b, zero_val, sin_b]), jnp.stack([zero_val, one_val, zero_val]), jnp.stack([-sin_b, zero_val, cos_b])])
    around_z = jnp.stack([jnp.stack([cos_c, -sin_c, zero_val]), jnp.stack([sin_c, cos_c, zero_val]), jnp.stack([zero_val, zero_val, one_val])])
    return jnp.dot(around_z, jnp.dot(around_y, around_x, precision=HIGHEST_PREC), precision=HIGHEST_PREC)

def harmonic_basis(direction):
    dir_x, dir_y, dir_z = (direction[0], direction[1], direction[2])
    dir_xx, dir_yy, dir_zz = (dir_x * dir_x, dir_y * dir_y, dir_z * dir_z)
    terms = [HARM_ZERO * jnp.ones_like(dir_x), -HARM_ONE * dir_y, HARM_ONE * dir_z, -HARM_ONE * dir_x, HARM_TWO[0] * dir_x * dir_y, HARM_TWO[1] * dir_y * dir_z, HARM_TWO[2] * (2.0 * dir_zz - dir_xx - dir_yy), HARM_TWO[3] * dir_x * dir_z, HARM_TWO[4] * (dir_xx - dir_yy), HARM_THREE[0] * dir_y * (3.0 * dir_xx - dir_yy), HARM_THREE[1] * dir_x * dir_y * dir_z, HARM_THREE[2] * dir_y * (4.0 * dir_zz - dir_xx - dir_yy), HARM_THREE[3] * dir_z * (2.0 * dir_zz - 3.0 * dir_xx - 3.0 * dir_yy), HARM_THREE[4] * dir_x * (4.0 * dir_zz - dir_xx - dir_yy), HARM_THREE[5] * dir_z * (dir_xx - dir_yy), HARM_THREE[6] * dir_x * (dir_xx - 3.0 * dir_yy)]
    return jnp.stack(terms)

def project(attr_rows, camera, focal_len, center_y):
    world_rot = rotation_of(camera)
    translate = jnp.stack([camera[3], camera[4], 5.0 + camera[5]])
    means = attr_rows[0:3]
    camera_space = jnp.dot(world_rot, means, precision=HIGHEST_PREC) + translate[:, None]
    inverse = 1.0 / camera_space[2]
    screen_u = focal_len * camera_space[0] * inverse + 128.0
    screen_v = focal_len * camera_space[1] * inverse + center_y
    scales = jnp.exp(attr_rows[3:6])
    quaternion = attr_rows[6:10] / jnp.sqrt(lax.optimization_barrier(jnp.sum(attr_rows[6:10] * attr_rows[6:10], axis=0)))
    q_r, q_x, q_y, q_z = (quaternion[0], quaternion[1], quaternion[2], quaternion[3])
    rotor = [[1.0 - 2.0 * (q_y * q_y + q_z * q_z), 2.0 * (q_x * q_y - q_r * q_z), 2.0 * (q_x * q_z + q_r * q_y)], [2.0 * (q_x * q_y + q_r * q_z), 1.0 - 2.0 * (q_x * q_x + q_z * q_z), 2.0 * (q_y * q_z - q_r * q_x)], [2.0 * (q_x * q_z - q_r * q_y), 2.0 * (q_y * q_z + q_r * q_x), 1.0 - 2.0 * (q_x * q_x + q_y * q_y)]]
    jac_zero = [focal_len * inverse, 0.0, -focal_len * camera_space[0] * inverse * inverse]
    jac_one = [0.0, focal_len * inverse, -focal_len * camera_space[1] * inverse * inverse]
    jacobian = [jac_zero, jac_one]
    mapped = []
    for outer in range(2):
        through = [sum((jacobian[outer][middle] * world_rot[middle, inner] for middle in range(3))) for inner in range(3)]
        mapped.append([sum((through[inner] * rotor[inner][column] for inner in range(3))) * scales[column] for column in range(3)])
    cov_aa = sum((mapped[0][column] * mapped[0][column] for column in range(3))) + 0.3
    cov_ab = sum((mapped[0][column] * mapped[1][column] for column in range(3)))
    cov_bb = sum((mapped[1][column] * mapped[1][column] for column in range(3))) + 0.3
    determinant = cov_aa * cov_bb - cov_ab * cov_ab
    opacity = jax.nn.sigmoid(attr_rows[10])
    centre = -jnp.dot(world_rot.T, translate, precision=HIGHEST_PREC)
    offset = means - centre[:, None]
    direction = offset / jnp.sqrt(lax.optimization_barrier(jnp.sum(offset * offset, axis=0)))
    harmonic = harmonic_basis(direction)
    coeffs = attr_rows[11:59].reshape(16, 3, attr_rows.shape[1])
    colour_rgb = jnp.maximum(lax.optimization_barrier(jnp.sum(harmonic[:, None, :] * coeffs, axis=0)) + 0.5, 0.0)
    firsts = jnp.stack([screen_u, screen_v, cov_bb / determinant, -cov_ab / determinant, cov_aa / determinant, opacity])
    return jnp.concatenate([firsts, colour_rgb], axis=0)

def tile_term(screen, tile_index, blocks, slots, target_tile):
    listed = jnp.take(screen, slots, axis=1)
    live_mask = (jnp.arange(slots.shape[0], dtype=jnp.int32) < blocks * BLOCK).astype(jnp.float32)
    pixels = jnp.arange(256, dtype=jnp.int32)
    pixel_x = (tile_index % 16 * 16 + pixels % 16).astype(jnp.float32)
    pixel_y = (tile_index // 16 * 16 + pixels // 16).astype(jnp.float32)
    delta_x = listed[0][None, :] - pixel_x[:, None]
    delta_y = listed[1][None, :] - pixel_y[:, None]
    exponent = -0.5 * (listed[2][None, :] * delta_x * delta_x + listed[4][None, :] * delta_y * delta_y) - listed[3][None, :] * delta_x * delta_y
    alphas = listed[5][None, :] * jnp.exp(exponent) * live_mask[None, :]
    log_keep = jnp.log1p(-alphas)
    before = jnp.cumsum(log_keep, axis=1) - log_keep
    weight = alphas * jnp.exp(before)
    render_rgb = jnp.einsum('cl,pl->cp', listed[6:9], weight, precision=HIGHEST_PREC)
    residual = render_rgb - target_tile
    return 0.5 * jnp.sum(residual * residual)

def render_loss(screen, tile_ids, tile_blocks, tile_lists, target):

    def per_tile(items):
        return tile_term(screen, items[0], items[1], items[2], items[3])
    terms = lax.map(jax.checkpoint(per_tile), (tile_ids, tile_blocks, tile_lists, target))
    return jnp.sum(terms)

def rate_table():
    return jnp.concatenate([jnp.full((3,), 0.00016, jnp.float32), jnp.full((3,), 0.005, jnp.float32), jnp.full((4,), 0.001, jnp.float32), jnp.full((1,), 0.025, jnp.float32), jnp.full((3,), 0.0025, jnp.float32), jnp.full((45,), 0.000125, jnp.float32)])

def adam_update(params, adam_m, adam_v, param_grad):
    first_new = BETA_ONE * adam_m + (1.0 - BETA_ONE) * param_grad
    second_new = BETA_TWO * adam_v + (1.0 - BETA_TWO) * param_grad * param_grad
    fix_one = 1.0 - BETA_ONE ** ADAM_STEP
    fix_two = 1.0 - BETA_TWO ** ADAM_STEP
    stepped = first_new / fix_one / (jnp.sqrt(second_new / fix_two) + ADAM_EPSILON)
    return (params - rate_table()[:, None] * stepped, first_new, second_new)

def reference(params, adam_m, adam_v, camera, target, tile_ids, tile_blocks, tile_lists, send_rows):
    focal_len, center_y = geometry(tile_ids.shape[0])

    def device_loss(weights, renderer):
        columns = (jnp.arange(N_SPACE, dtype=jnp.int32)[:, None] * G_DEV + send_rows[:, renderer, :]).reshape(-1)
        received = jnp.take(weights, columns, axis=1)
        screen = project(received, camera, focal_len, center_y)
        start = (renderer * TILE_DEV).astype(jnp.int32)
        return render_loss(screen, lax.dynamic_slice_in_dim(tile_ids, start, TILE_DEV), lax.dynamic_slice_in_dim(tile_blocks, start, TILE_DEV), lax.dynamic_slice_in_dim(tile_lists, start, TILE_DEV), lax.dynamic_slice_in_dim(target, start, TILE_DEV))

    def total_loss(weights):

        def one_device(renderer):
            return device_loss(weights, renderer)
        return jnp.sum(lax.map(one_device, jnp.arange(N_SPACE, dtype=jnp.int32)))
    param_grad = jax.grad(total_loss)(params)
    return adam_update(params, adam_m, adam_v, param_grad)
```

```python
import functools

import jax
import jax.numpy as jnp
from jax import lax
from jax.experimental import pallas as pl
from jax.experimental.pallas import tpu as pltpu
from jax.sharding import PartitionSpec as P

BLOCK = 256
ADAM_STEP = 10
BETA_ONE = 0.9
BETA_TWO = 0.999
ADAM_EPSILON = 1e-15
HARM_ZERO = 0.28209479177387814
HARM_ONE = 0.4886025119029199
HARM_TWO = (
    1.0925484305920792,
    -1.0925484305920792,
    0.31539156525252005,
    -1.0925484305920792,
    0.5462742152960396,
)
HARM_THREE = (
    -0.5900435899266435,
    2.890611442640554,
    -0.4570457994644658,
    0.3731763325901154,
    -0.4570457994644658,
    1.445305721320277,
    -0.5900435899266435,
)
ATTRS = 59
SCREEN = 9
CHUNK = 1024
LANES = 128
F32 = jnp.float32
BF16 = jnp.bfloat16
VMEM_LIMIT = 56 * 1024 * 1024


def view_of(cam_ref):
    def splat(index):
        return jnp.full((8, LANES), cam_ref[index], F32)

    cos_a, sin_a = jnp.cos(splat(0)), jnp.sin(splat(0))
    cos_b, sin_b = jnp.cos(splat(1)), jnp.sin(splat(1))
    cos_c, sin_c = jnp.cos(splat(2)), jnp.sin(splat(2))
    world = [
        [
            cos_c * cos_b,
            cos_c * sin_b * sin_a - sin_c * cos_a,
            cos_c * sin_b * cos_a + sin_c * sin_a,
        ],
        [
            sin_c * cos_b,
            sin_c * sin_b * sin_a + cos_c * cos_a,
            sin_c * sin_b * cos_a - cos_c * sin_a,
        ],
        [-sin_b, cos_b * sin_a, cos_b * cos_a],
    ]
    translate = [splat(3), splat(4), 5.0 + splat(5)]
    centre = [-sum(world[k][i] * translate[k] for k in range(3)) for i in range(3)]
    return [world[i][j] for i in range(3) for j in range(3)] + translate + centre


def harmonic_basis(dir_x, dir_y, dir_z):
    dir_xx, dir_yy, dir_zz = (dir_x * dir_x, dir_y * dir_y, dir_z * dir_z)
    return [
        jnp.full_like(dir_x, HARM_ZERO),
        -HARM_ONE * dir_y,
        HARM_ONE * dir_z,
        -HARM_ONE * dir_x,
        HARM_TWO[0] * dir_x * dir_y,
        HARM_TWO[1] * dir_y * dir_z,
        HARM_TWO[2] * (2.0 * dir_zz - dir_xx - dir_yy),
        HARM_TWO[3] * dir_x * dir_z,
        HARM_TWO[4] * (dir_xx - dir_yy),
        HARM_THREE[0] * dir_y * (3.0 * dir_xx - dir_yy),
        HARM_THREE[1] * dir_x * dir_y * dir_z,
        HARM_THREE[2] * dir_y * (4.0 * dir_zz - dir_xx - dir_yy),
        HARM_THREE[3] * dir_z * (2.0 * dir_zz - 3.0 * dir_xx - 3.0 * dir_yy),
        HARM_THREE[4] * dir_x * (4.0 * dir_zz - dir_xx - dir_yy),
        HARM_THREE[5] * dir_z * (dir_xx - dir_yy),
        HARM_THREE[6] * dir_x * (dir_xx - 3.0 * dir_yy),
    ]


def project(attr, view, focal_len, center_y):
    world = [view[0:3], view[3:6], view[6:9]]
    translate, centre = view[9:12], view[12:15]
    cam = [sum(world[i][k] * attr[k] for k in range(3)) + translate[i] for i in range(3)]
    inverse = 1.0 / cam[2]
    screen_u = focal_len * cam[0] * inverse + 128.0
    screen_v = focal_len * cam[1] * inverse + center_y
    scales = [jnp.exp(attr[3 + k]) for k in range(3)]
    norm = lax.rsqrt(sum(attr[6 + k] * attr[6 + k] for k in range(4)))
    q_r, q_x, q_y, q_z = [attr[6 + k] * norm for k in range(4)]
    rotor = [
        [
            1.0 - 2.0 * (q_y * q_y + q_z * q_z),
            2.0 * (q_x * q_y - q_r * q_z),
            2.0 * (q_x * q_z + q_r * q_y),
        ],
        [
            2.0 * (q_x * q_y + q_r * q_z),
            1.0 - 2.0 * (q_x * q_x + q_z * q_z),
            2.0 * (q_y * q_z - q_r * q_x),
        ],
        [
            2.0 * (q_x * q_z - q_r * q_y),
            2.0 * (q_y * q_z + q_r * q_x),
            1.0 - 2.0 * (q_x * q_x + q_y * q_y),
        ],
    ]
    near = focal_len * inverse
    far = [-near * cam[outer] * inverse for outer in range(2)]
    mapped = []
    for outer in range(2):
        through = [near * world[outer][k] + far[outer] * world[2][k] for k in range(3)]
        mapped.append(
            [sum(through[k] * rotor[k][col] for k in range(3)) * scales[col] for col in range(3)]
        )
    cov_aa = sum(mapped[0][col] * mapped[0][col] for col in range(3)) + 0.3
    cov_ab = sum(mapped[0][col] * mapped[1][col] for col in range(3))
    cov_bb = sum(mapped[1][col] * mapped[1][col] for col in range(3)) + 0.3
    over = 1.0 / (cov_aa * cov_bb - cov_ab * cov_ab)
    opacity = 1.0 / (1.0 + jnp.exp(-attr[10]))
    offset = [attr[k] - centre[k] for k in range(3)]
    length = lax.rsqrt(sum(offset[k] * offset[k] for k in range(3)))
    basis = harmonic_basis(*[offset[k] * length for k in range(3)])
    colour = [
        jnp.maximum(sum(basis[k] * attr[11 + 3 * k + c] for k in range(16)) + 0.5, 0.0)
        for c in range(3)
    ]
    return [screen_u, screen_v, cov_bb * over, -cov_ab * over, cov_aa * over, opacity] + colour


def split(value, parts):
    out = []
    for index in range(parts):
        piece = value.astype(BF16)
        out.append(piece)
        if index + 1 < parts:
            value = value - piece.astype(F32)
    return out


def low_one_hot(index):
    rows = lax.broadcasted_iota(jnp.int32, (LANES, index.shape[1]), 0)
    return jnp.where(rows == (index & (LANES - 1)), 1.0, 0.0)


def high_match(index, groups):
    rows = lax.broadcasted_iota(jnp.int32, (groups, index.shape[1]), 0)
    return rows == (index >> 7)


def gather_columns(pieces, index, groups):
    hot = low_one_hot(index).astype(BF16)
    count = pieces.shape[1] // LANES
    hots = jnp.concatenate([hot] * count, axis=0)
    picked = jnp.dot(pieces, hots, preferred_element_type=F32)
    match = high_match(index, groups)
    return [
        jnp.sum(
            jnp.where(match, picked[r * groups : (r + 1) * groups], 0.0), axis=0, keepdims=True
        )
        for r in range(SCREEN)
    ]


def scatter_columns(rows, index, groups):
    hot = low_one_hot(index).astype(BF16)
    match = jnp.where(high_match(index, groups), 1.0, 0.0).astype(BF16)
    total = None
    for piece in split(rows, 2):
        left = jnp.concatenate([piece[r : r + 1] * match for r in range(SCREEN)], axis=0)
        part = lax.dot_general(
            left, hot, (((1,), (1,)), ((), ())), preferred_element_type=F32
        )
        total = part if total is None else total + part
    return total


def owner_kernel(sizes, params_ref, cam_ref, rows_ref, out_ref, view_ref, attr_ref, screen_ref):
    spaces, capacity, groups, focal_len, center_y = sizes
    step = pl.program_id(0)

    @pl.when(step == 0)
    def _():
        for k, value in enumerate(view_of(cam_ref)):
            view_ref[k] = value

    for q in range(8):
        attr_ref[pl.ds(q, ATTRS, stride=8), :] = params_ref[:, q * LANES : (q + 1) * LANES]
    view = [view_ref[k] for k in range(15)]
    attr = [attr_ref[8 * k : 8 * k + 8, :] for k in range(ATTRS)]
    values = project(attr, view, focal_len, center_y)
    for r in range(SCREEN):
        screen_ref[pl.ds(pl.multiple_of(r * groups + step * 8, 8), 8), :] = values[r]

    @pl.when(step == pl.num_programs(0) - 1)
    def _():
        pieces = jnp.concatenate(split(screen_ref[...], 3), axis=1)

        def send(d, carry):
            got = gather_columns(pieces, rows_ref[pl.ds(d, 1), :], groups)
            out_ref[d] = jnp.concatenate(got, axis=0)
            return carry

        lax.fori_loop(0, spaces, send, 0)


def render_kernel(
    sizes,
    recv_ref,
    lists_ref,
    target_ref,
    ids_ref,
    blocks_ref,
    out_ref,
    pieces_ref,
    lines_ref,
    alpha_ref,
    weight_ref,
    total_ref,
):
    spaces, capacity, groups, tiles, length = sizes
    per = capacity // LANES
    for r in range(SCREEN):
        for s in range(spaces):
            for k in range(per):
                row = r * groups + s * per + k
                lines_ref[row : row + 1, :] = recv_ref[s, r : r + 1, k * LANES : (k + 1) * LANES]
    for k, piece in enumerate(split(lines_ref[...], 3)):
        pieces_ref[:, k * LANES : (k + 1) * LANES] = piece
    total_ref[...] = jnp.zeros_like(total_ref)

    earlier = lax.broadcasted_iota(jnp.int32, (BLOCK, BLOCK), 0)
    later = lax.broadcasted_iota(jnp.int32, (BLOCK, BLOCK), 1)
    before = jnp.where(earlier < later, 1.0, 0.0).astype(BF16)
    upto = jnp.where(earlier <= later, 1.0, 0.0).astype(BF16)
    pixel = lax.broadcasted_iota(jnp.int32, (8, 256), 1)
    which = lax.broadcasted_iota(jnp.int32, (8, 256), 0)
    local_x = (pixel % 16 - 8).astype(F32)
    local_y = (pixel // 16 - 8).astype(F32)
    power = jnp.where(which == 0, 1.0, 0.0)
    for row, term in enumerate(
        [local_x, local_y, local_x * local_x, local_x * local_y, local_y * local_y]
    ):
        power = jnp.where(which == row + 1, term, power)
    power = power.astype(BF16)
    offsets = (lax.broadcasted_iota(jnp.int32, (16, BLOCK), 0) - 8).astype(F32)

    def prefix(value, ones):
        high, low = split(value, 2)
        return jnp.dot(high, ones, preferred_element_type=F32) + jnp.dot(
            low, ones, preferred_element_type=F32
        )

    def tile(i, carry):
        tile_id = ids_ref[i]
        live = blocks_ref[i] * BLOCK
        index_row = lists_ref[pl.ds(i, 1), :]
        base_x = ((tile_id % 16) * 16 + 8).astype(F32)
        base_y = ((tile_id // 16) * 16 + 8).astype(F32)
        kept = []
        run = jnp.zeros((256, 1), F32)
        render = jnp.zeros((8, 256), F32)
        for b in range(length // BLOCK):
            cut = slice(b * BLOCK, (b + 1) * BLOCK)
            index = index_row[:, cut]
            got = gather_columns(pieces_ref[...], index, groups)
            spot = lax.broadcasted_iota(jnp.int32, (1, BLOCK), 1) + b * BLOCK
            shown = jnp.where(spot < live, got[5], 0.0)
            local_u = got[0] - base_x
            local_v = got[1] - base_y
            delta_x = local_u - offsets
            delta_y = local_v - offsets
            part_x = -0.5 * got[2] * delta_x * delta_x
            part_y = -0.5 * got[4] * delta_y * delta_y
            cross = -got[3] * delta_y
            alpha = jnp.concatenate(
                [
                    shown
                    * jnp.exp(
                        part_x + part_y[y : y + 1, :] + delta_x * cross[y : y + 1, :]
                    )
                    for y in range(16)
                ],
                axis=0,
            )
            keep = jnp.log(1.0 - alpha)
            ahead = prefix(keep, before) + run
            run = ahead[:, BLOCK - 1 :] + keep[:, BLOCK - 1 :]
            weight = alpha * jnp.exp(ahead)
            colour = jnp.concatenate(got[6:9] + [jnp.zeros((5, BLOCK), F32)], axis=0)
            alpha_ref[:, cut] = alpha
            weight_ref[:, cut] = weight
            high, low = split(weight, 2)
            col_high, col_low = split(colour, 2)
            nt = (((1,), (1,)), ((), ()))
            for left, right in ((col_high, high), (col_low, high), (col_high, low)):
                render = render + lax.dot_general(left, right, nt, preferred_element_type=F32)
            kept.append((index, got, local_u, local_v, col_high, col_low))

        residual = render - jnp.concatenate([target_ref[i], jnp.zeros((5, 256), F32)], axis=0)
        res_high, res_low = split(residual, 2)
        turned = residual.T
        turn_high, turn_low = split(turned, 2)
        whole = jnp.sum((render * residual).T, axis=1, keepdims=True)
        for b in range(length // BLOCK):
            cut = slice(b * BLOCK, (b + 1) * BLOCK)
            index, got, local_u, local_v, col_high, col_low = kept[b]
            alpha = alpha_ref[:, cut]
            weight = weight_ref[:, cut]
            slope = (
                jnp.dot(turn_high, col_high, preferred_element_type=F32)
                + jnp.dot(turn_low, col_high, preferred_element_type=F32)
                + jnp.dot(turn_high, col_low, preferred_element_type=F32)
            )
            moved = slope * weight
            rest = whole - prefix(moved, upto)
            whole = rest[:, BLOCK - 1 :]
            push = moved - rest * (alpha / (1.0 - alpha))
            high, low = split(push, 2)
            moment = jnp.dot(power, high, preferred_element_type=F32) + jnp.dot(
                power, low, preferred_element_type=F32
            )
            high, low = split(weight, 2)
            hue = (
                jnp.dot(res_high, high, preferred_element_type=F32)
                + jnp.dot(res_low, high, preferred_element_type=F32)
                + jnp.dot(res_high, low, preferred_element_type=F32)
            )
            m_0, m_x, m_y, m_xx, m_xy, m_yy = [moment[k : k + 1] for k in range(6)]
            s_x = local_u * m_0 - m_x
            s_y = local_v * m_0 - m_y
            s_xx = local_u * (local_u * m_0 - 2.0 * m_x) + m_xx
            s_yy = local_v * (local_v * m_0 - 2.0 * m_y) + m_yy
            s_xy = local_u * s_y - local_v * m_x + m_xy
            back = jnp.concatenate(
                [
                    -(got[2] * s_x + got[3] * s_y),
                    -(got[4] * s_y + got[3] * s_x),
                    -0.5 * s_xx,
                    -s_xy,
                    -0.5 * s_yy,
                    m_0 / got[5],
                    hue[0:3],
                ],
                axis=0,
            )
            total_ref[...] += scatter_columns(back, index, groups)
        return carry

    lax.fori_loop(0, tiles, tile, 0)
    for r in range(SCREEN):
        for s in range(spaces):
            for k in range(per):
                row = r * groups + s * per + k
                out_ref[s, r : r + 1, k * LANES : (k + 1) * LANES] = total_ref[row : row + 1, :]


def update_kernel(
    sizes,
    params_ref,
    m_ref,
    v_ref,
    cam_ref,
    rows_ref,
    back_ref,
    new_params_ref,
    new_m_ref,
    new_v_ref,
    view_ref,
    attr_ref,
    total_ref,
):
    spaces, capacity, groups, focal_len, center_y = sizes
    step = pl.program_id(0)

    @pl.when(step == 0)
    def _():
        for k, value in enumerate(view_of(cam_ref)):
            view_ref[k] = value
        total_ref[...] = jnp.zeros_like(total_ref)

        def add(d, carry):
            total_ref[...] += scatter_columns(back_ref[d], rows_ref[pl.ds(d, 1), :], groups)
            return carry

        lax.fori_loop(0, spaces, add, 0)

    for q in range(8):
        attr_ref[pl.ds(q, ATTRS, stride=8), :] = params_ref[:, q * LANES : (q + 1) * LANES]
    view = [view_ref[k] for k in range(15)]
    attr = [attr_ref[8 * k : 8 * k + 8, :] for k in range(ATTRS)]
    slopes = [
        total_ref[pl.ds(pl.multiple_of(r * groups + step * 8, 8), 8), :] for r in range(SCREEN)
    ]
    _, pull = jax.vjp(lambda a: project(a, view, focal_len, center_y), attr)
    (grads,) = pull(slopes)
    for k in range(ATTRS):
        attr_ref[8 * k : 8 * k + 8, :] = grads[k]

    row = lax.broadcasted_iota(jnp.int32, (ATTRS, LANES), 0)
    rate = jnp.full((ATTRS, LANES), 0.000125, F32)
    for end, value in ((14, 0.0025), (11, 0.025), (10, 0.001), (6, 0.005), (3, 0.00016)):
        rate = jnp.where(row < end, value, rate)
    rate = rate * (1.0 / (1.0 - BETA_ONE**ADAM_STEP))
    fix_two = 1.0 / (1.0 - BETA_TWO**ADAM_STEP)
    for q in range(8):
        cut = slice(q * LANES, (q + 1) * LANES)
        grad = attr_ref[pl.ds(q, ATTRS, stride=8), :]
        first = BETA_ONE * m_ref[:, cut] + (1.0 - BETA_ONE) * grad
        second = BETA_TWO * v_ref[:, cut] + (1.0 - BETA_TWO) * grad * grad
        new_m_ref[:, cut] = first
        new_v_ref[:, cut] = second
        new_params_ref[:, cut] = params_ref[:, cut] - rate * first / (
            jnp.sqrt(second * fix_two) + ADAM_EPSILON
        )


def body(params, adam_m, adam_v, camera, target, tile_ids, tile_blocks, tile_lists, send_rows):
    spaces, capacity = send_rows.shape[1:]
    tiles, length = tile_lists.shape
    count = params.shape[1]
    tiles_all = tiles * spaces
    focal_len, center_y = max(256, tiles_all) * 5.0 / 3.0, tiles_all * 0.5
    groups = count // LANES
    heard = spaces * capacity // LANES
    rows = send_rows[0]
    steps = count // CHUNK
    vmem = pl.BlockSpec(memory_space=pltpu.VMEM)
    smem = pl.BlockSpec(memory_space=pltpu.SMEM)
    chunk = pl.BlockSpec((ATTRS, CHUNK), lambda i: (0, i))
    limits = pltpu.CompilerParams(vmem_limit_bytes=VMEM_LIMIT)
    owner_sizes = (spaces, capacity, groups, focal_len, center_y)
    packet = jax.ShapeDtypeStruct((spaces, SCREEN, capacity), F32)

    outgoing = pl.pallas_call(
        functools.partial(owner_kernel, owner_sizes),
        grid=(steps,),
        in_specs=[chunk, smem, vmem],
        out_specs=vmem,
        out_shape=packet,
        scratch_shapes=[
            pltpu.VMEM((15, 8, LANES), F32),
            pltpu.VMEM((8 * ATTRS, LANES), F32),
            pltpu.VMEM((SCREEN * groups, LANES), F32),
        ],
        compiler_params=limits,
        name="project_and_pick",
    )(params, camera, rows)
    arrived = lax.all_to_all(outgoing, "space", split_axis=0, concat_axis=0, tiled=True)
    slopes = pl.pallas_call(
        functools.partial(render_kernel, (spaces, capacity, heard, tiles, length)),
        in_specs=[vmem, vmem, vmem, smem, smem],
        out_specs=vmem,
        out_shape=packet,
        scratch_shapes=[
            pltpu.VMEM((SCREEN * heard, 3 * LANES), BF16),
            pltpu.VMEM((SCREEN * heard, LANES), F32),
            pltpu.VMEM((256, length), F32),
            pltpu.VMEM((256, length), F32),
            pltpu.VMEM((SCREEN * heard, LANES), F32),
        ],
        compiler_params=limits,
        name="render_and_back",
    )(arrived, tile_lists, target, tile_ids, tile_blocks)
    returned = lax.all_to_all(slopes, "space", split_axis=0, concat_axis=0, tiled=True)
    whole = jax.ShapeDtypeStruct(params.shape, F32)
    return pl.pallas_call(
        functools.partial(update_kernel, owner_sizes),
        grid=(steps,),
        in_specs=[chunk, chunk, chunk, smem, vmem, vmem],
        out_specs=[chunk, chunk, chunk],
        out_shape=[whole, whole, whole],
        scratch_shapes=[
            pltpu.VMEM((15, 8, LANES), F32),
            pltpu.VMEM((8 * ATTRS, LANES), F32),
            pltpu.VMEM((SCREEN * groups, LANES), F32),
        ],
        compiler_params=limits,
        name="gradient_and_step",
    )(params, adam_m, adam_v, camera, rows, returned)


def solution(mesh):
    wide = P(None, ("groups", "space"))
    tiles = ("groups", "space")
    return jax.shard_map(
        lambda *args: tuple(body(*args)),
        mesh=mesh,
        in_specs=(
            wide,
            wide,
            wide,
            P("groups"),
            P(tiles, None, None),
            P(tiles),
            P(tiles),
            P(tiles, None),
            P(tiles, None, None),
        ),
        out_specs=(wide, wide, wide),
        check_vma=False,
    )
```

```python
import functools

import jax
import jax.numpy as jnp
from jax import lax
from jax.experimental import pallas as pl
from jax.experimental.pallas import tpu as pltpu
from jax.sharding import PartitionSpec as P

BLOCK = 256
ADAM_STEP = 10
BETA_ONE = 0.9
BETA_TWO = 0.999
ADAM_EPSILON = 1e-15
HARM_ZERO = 0.28209479177387814
HARM_ONE = 0.4886025119029199
HARM_TWO = (
    1.0925484305920792,
    -1.0925484305920792,
    0.31539156525252005,
    -1.0925484305920792,
    0.5462742152960396,
)
HARM_THREE = (
    -0.5900435899266435,
    2.890611442640554,
    -0.4570457994644658,
    0.3731763325901154,
    -0.4570457994644658,
    1.445305721320277,
    -0.5900435899266435,
)
ATTRS = 59
SCREEN = 9
CHUNK = 1024
LANES = 128
F32 = jnp.float32
BF16 = jnp.bfloat16
VMEM_LIMIT = 56 * 1024 * 1024


def view_of(cam_ref):
    def splat(index):
        return jnp.full((8, LANES), cam_ref[index], F32)

    cos_a, sin_a = jnp.cos(splat(0)), jnp.sin(splat(0))
    cos_b, sin_b = jnp.cos(splat(1)), jnp.sin(splat(1))
    cos_c, sin_c = jnp.cos(splat(2)), jnp.sin(splat(2))
    world = [
        [
            cos_c * cos_b,
            cos_c * sin_b * sin_a - sin_c * cos_a,
            cos_c * sin_b * cos_a + sin_c * sin_a,
        ],
        [
            sin_c * cos_b,
            sin_c * sin_b * sin_a + cos_c * cos_a,
            sin_c * sin_b * cos_a - cos_c * sin_a,
        ],
        [-sin_b, cos_b * sin_a, cos_b * cos_a],
    ]
    translate = [splat(3), splat(4), 5.0 + splat(5)]
    centre = [-sum(world[k][i] * translate[k] for k in range(3)) for i in range(3)]
    return [world[i][j] for i in range(3) for j in range(3)] + translate + centre


def harmonic_basis(dir_x, dir_y, dir_z):
    dir_xx, dir_yy, dir_zz = (dir_x * dir_x, dir_y * dir_y, dir_z * dir_z)
    return [
        jnp.full_like(dir_x, HARM_ZERO),
        -HARM_ONE * dir_y,
        HARM_ONE * dir_z,
        -HARM_ONE * dir_x,
        HARM_TWO[0] * dir_x * dir_y,
        HARM_TWO[1] * dir_y * dir_z,
        HARM_TWO[2] * (2.0 * dir_zz - dir_xx - dir_yy),
        HARM_TWO[3] * dir_x * dir_z,
        HARM_TWO[4] * (dir_xx - dir_yy),
        HARM_THREE[0] * dir_y * (3.0 * dir_xx - dir_yy),
        HARM_THREE[1] * dir_x * dir_y * dir_z,
        HARM_THREE[2] * dir_y * (4.0 * dir_zz - dir_xx - dir_yy),
        HARM_THREE[3] * dir_z * (2.0 * dir_zz - 3.0 * dir_xx - 3.0 * dir_yy),
        HARM_THREE[4] * dir_x * (4.0 * dir_zz - dir_xx - dir_yy),
        HARM_THREE[5] * dir_z * (dir_xx - dir_yy),
        HARM_THREE[6] * dir_x * (dir_xx - 3.0 * dir_yy),
    ]


def project(attr, view, focal_len, center_y):
    world = [view[0:3], view[3:6], view[6:9]]
    translate, centre = view[9:12], view[12:15]
    cam = [sum(world[i][k] * attr[k] for k in range(3)) + translate[i] for i in range(3)]
    inverse = 1.0 / cam[2]
    screen_u = focal_len * cam[0] * inverse + 128.0
    screen_v = focal_len * cam[1] * inverse + center_y
    scales = [jnp.exp(attr[3 + k]) for k in range(3)]
    norm = lax.rsqrt(sum(attr[6 + k] * attr[6 + k] for k in range(4)))
    q_r, q_x, q_y, q_z = [attr[6 + k] * norm for k in range(4)]
    rotor = [
        [
            1.0 - 2.0 * (q_y * q_y + q_z * q_z),
            2.0 * (q_x * q_y - q_r * q_z),
            2.0 * (q_x * q_z + q_r * q_y),
        ],
        [
            2.0 * (q_x * q_y + q_r * q_z),
            1.0 - 2.0 * (q_x * q_x + q_z * q_z),
            2.0 * (q_y * q_z - q_r * q_x),
        ],
        [
            2.0 * (q_x * q_z - q_r * q_y),
            2.0 * (q_y * q_z + q_r * q_x),
            1.0 - 2.0 * (q_x * q_x + q_y * q_y),
        ],
    ]
    near = focal_len * inverse
    far = [-near * cam[outer] * inverse for outer in range(2)]
    mapped = []
    for outer in range(2):
        through = [near * world[outer][k] + far[outer] * world[2][k] for k in range(3)]
        mapped.append(
            [sum(through[k] * rotor[k][col] for k in range(3)) * scales[col] for col in range(3)]
        )
    cov_aa = sum(mapped[0][col] * mapped[0][col] for col in range(3)) + 0.3
    cov_ab = sum(mapped[0][col] * mapped[1][col] for col in range(3))
    cov_bb = sum(mapped[1][col] * mapped[1][col] for col in range(3)) + 0.3
    over = 1.0 / (cov_aa * cov_bb - cov_ab * cov_ab)
    opacity = 1.0 / (1.0 + jnp.exp(-attr[10]))
    offset = [attr[k] - centre[k] for k in range(3)]
    length = lax.rsqrt(sum(offset[k] * offset[k] for k in range(3)))
    basis = harmonic_basis(*[offset[k] * length for k in range(3)])
    colour = [
        jnp.maximum(sum(basis[k] * attr[11 + 3 * k + c] for k in range(16)) + 0.5, 0.0)
        for c in range(3)
    ]
    return [screen_u, screen_v, cov_bb * over, -cov_ab * over, cov_aa * over, opacity] + colour


def split(value, parts):
    out = []
    for index in range(parts):
        piece = value.astype(BF16)
        out.append(piece)
        if index + 1 < parts:
            value = value - piece.astype(F32)
    return out


def low_one_hot(index):
    rows = lax.broadcasted_iota(jnp.int32, (LANES, index.shape[1]), 0)
    return jnp.where(rows == (index & (LANES - 1)), 1.0, 0.0)


def high_match(index, groups):
    rows = lax.broadcasted_iota(jnp.int32, (groups, index.shape[1]), 0)
    return rows == (index >> 7)


def gather_columns(pieces, index, groups):
    hot = low_one_hot(index).astype(BF16)
    count = pieces.shape[1] // LANES
    hots = jnp.concatenate([hot] * count, axis=0)
    picked = jnp.dot(pieces, hots, preferred_element_type=F32)
    match = high_match(index, groups)
    return [
        jnp.sum(
            jnp.where(match, picked[r * groups : (r + 1) * groups], 0.0), axis=0, keepdims=True
        )
        for r in range(SCREEN)
    ]


def scatter_columns(rows, index, groups):
    hot = low_one_hot(index).astype(BF16)
    match = jnp.where(high_match(index, groups), 1.0, 0.0).astype(BF16)
    total = None
    for piece in split(rows, 2):
        left = jnp.concatenate([piece[r : r + 1] * match for r in range(SCREEN)], axis=0)
        part = lax.dot_general(
            left, hot, (((1,), (1,)), ((), ())), preferred_element_type=F32
        )
        total = part if total is None else total + part
    return total


def owner_kernel(sizes, params_ref, cam_ref, screen_ref, view_ref, attr_ref):
    groups, focal_len, center_y = sizes
    step = pl.program_id(0)

    @pl.when(step == 0)
    def _():
        for k, value in enumerate(view_of(cam_ref)):
            view_ref[k] = value

    for q in range(8):
        attr_ref[pl.ds(q, ATTRS, stride=8), :] = params_ref[:, q * LANES : (q + 1) * LANES]
    view = [view_ref[k] for k in range(15)]
    attr = [attr_ref[8 * k : 8 * k + 8, :] for k in range(ATTRS)]
    values = project(attr, view, focal_len, center_y)
    for r in range(SCREEN):
        screen_ref[pl.ds(pl.multiple_of(r * groups + step * 8, 8), 8), :] = values[r]


def greet(spaces):
    me = lax.axis_index("space")
    barrier = pltpu.get_barrier_semaphore()

    def signal(t, carry):
        pl.semaphore_signal(
            barrier,
            inc=1,
            device_id={"space": lax.rem(me + t, spaces)},
            device_id_type=pl.DeviceIdType.MESH,
        )
        return carry

    lax.fori_loop(1, spaces, signal, 0)
    pl.semaphore_wait(barrier, spaces - 1)


def packet_copy(kept_ref, land_ref, send_sem, recv_sem, source, target):
    return pltpu.make_async_remote_copy(
        src_ref=kept_ref.at[target],
        dst_ref=land_ref.at[source],
        send_sem=send_sem.at[target],
        recv_sem=recv_sem.at[source],
        device_id={"space": target},
        device_id_type=pl.DeviceIdType.MESH,
    )


def send_kernel(
    sizes, screen_ref, rows_ref, lines_ref, pieces_ref, kept_ref, land_ref, send_sem, recv_sem
):
    spaces, capacity, groups = sizes
    per = capacity // LANES
    heard = spaces * per
    me = lax.axis_index("space")
    for k, piece in enumerate(split(screen_ref[...], 3)):
        pieces_ref[:, k * LANES : (k + 1) * LANES] = piece

    def pick(d):
        got = gather_columns(pieces_ref[...], rows_ref[pl.ds(d, 1), :], groups)
        return jnp.concatenate(got, axis=0)

    def unpack(s, packet):
        for r in range(SCREEN):
            for k in range(per):
                lines_ref[pl.ds(r * heard + s * per + k, 1), :] = packet[
                    r : r + 1, k * LANES : (k + 1) * LANES
                ]

    greet(spaces)

    def send(t, carry):
        d = lax.rem(me + t, spaces)
        kept_ref[d] = pick(d)
        packet_copy(kept_ref, land_ref, send_sem, recv_sem, me, d).start()
        return carry

    lax.fori_loop(1, spaces, send, 0)
    unpack(me, pick(me))

    def take(t, carry):
        s = lax.rem(me + spaces - t, spaces)
        packet_copy(kept_ref, land_ref, send_sem, recv_sem, s, s).wait_recv()
        unpack(s, land_ref[s])
        return carry

    lax.fori_loop(1, spaces, take, 0)

    def done(t, carry):
        d = lax.rem(me + t, spaces)
        packet_copy(kept_ref, land_ref, send_sem, recv_sem, me, d).wait_send()
        return carry

    lax.fori_loop(1, spaces, done, 0)


def return_kernel(
    sizes, slopes_ref, rows_ref, out_ref, kept_ref, land_ref, send_sem, recv_sem
):
    spaces, capacity, groups = sizes
    per = capacity // LANES
    heard = spaces * per
    me = lax.axis_index("space")

    def pack(d):
        for r in range(SCREEN):
            for k in range(per):
                kept_ref[d, r : r + 1, k * LANES : (k + 1) * LANES] = slopes_ref[
                    pl.ds(r * heard + d * per + k, 1), :
                ]

    greet(spaces)

    def send(t, carry):
        d = lax.rem(me + t, spaces)
        pack(d)
        packet_copy(kept_ref, land_ref, send_sem, recv_sem, me, d).start()
        return carry

    lax.fori_loop(1, spaces, send, 0)
    pack(me)
    out_ref[...] = scatter_columns(kept_ref[me], rows_ref[pl.ds(me, 1), :], groups)

    def take(t, carry):
        s = lax.rem(me + spaces - t, spaces)
        packet_copy(kept_ref, land_ref, send_sem, recv_sem, s, s).wait_recv()
        out_ref[...] += scatter_columns(land_ref[s], rows_ref[pl.ds(s, 1), :], groups)
        return carry

    lax.fori_loop(1, spaces, take, 0)

    def done(t, carry):
        d = lax.rem(me + t, spaces)
        packet_copy(kept_ref, land_ref, send_sem, recv_sem, me, d).wait_send()
        return carry

    lax.fori_loop(1, spaces, done, 0)


def render_kernel(
    sizes,
    lines_ref,
    lists_ref,
    target_ref,
    ids_ref,
    blocks_ref,
    total_ref,
    pieces_ref,
    alpha_ref,
    weight_ref,
):
    groups, tiles, length = sizes
    for k, piece in enumerate(split(lines_ref[...], 3)):
        pieces_ref[:, k * LANES : (k + 1) * LANES] = piece
    total_ref[...] = jnp.zeros_like(total_ref)

    earlier = lax.broadcasted_iota(jnp.int32, (BLOCK, BLOCK), 0)
    later = lax.broadcasted_iota(jnp.int32, (BLOCK, BLOCK), 1)
    before = jnp.where(earlier < later, 1.0, 0.0).astype(BF16)
    upto = jnp.where(earlier <= later, 1.0, 0.0).astype(BF16)
    pixel = lax.broadcasted_iota(jnp.int32, (8, 256), 1)
    which = lax.broadcasted_iota(jnp.int32, (8, 256), 0)
    local_x = (pixel % 16 - 8).astype(F32)
    local_y = (pixel // 16 - 8).astype(F32)
    power = jnp.where(which == 0, 1.0, 0.0)
    for row, term in enumerate(
        [local_x, local_y, local_x * local_x, local_x * local_y, local_y * local_y]
    ):
        power = jnp.where(which == row + 1, term, power)
    power = power.astype(BF16)
    offsets = (lax.broadcasted_iota(jnp.int32, (16, BLOCK), 0) - 8).astype(F32)

    def prefix(value, ones):
        high, low = split(value, 2)
        return jnp.dot(high, ones, preferred_element_type=F32) + jnp.dot(
            low, ones, preferred_element_type=F32
        )

    def tile(i, carry):
        tile_id = ids_ref[i]
        live = blocks_ref[i] * BLOCK
        index_row = lists_ref[pl.ds(i, 1), :]
        base_x = ((tile_id % 16) * 16 + 8).astype(F32)
        base_y = ((tile_id // 16) * 16 + 8).astype(F32)
        kept = []
        run = jnp.zeros((256, 1), F32)
        render = jnp.zeros((8, 256), F32)
        for b in range(length // BLOCK):
            cut = slice(b * BLOCK, (b + 1) * BLOCK)
            index = index_row[:, cut]
            got = gather_columns(pieces_ref[...], index, groups)
            spot = lax.broadcasted_iota(jnp.int32, (1, BLOCK), 1) + b * BLOCK
            shown = jnp.where(spot < live, got[5], 0.0)
            local_u = got[0] - base_x
            local_v = got[1] - base_y
            delta_x = local_u - offsets
            delta_y = local_v - offsets
            part_x = -0.5 * got[2] * delta_x * delta_x
            part_y = -0.5 * got[4] * delta_y * delta_y
            cross = -got[3] * delta_y
            alpha = jnp.concatenate(
                [
                    shown
                    * jnp.exp(
                        part_x + part_y[y : y + 1, :] + delta_x * cross[y : y + 1, :]
                    )
                    for y in range(16)
                ],
                axis=0,
            )
            keep = jnp.log(1.0 - alpha)
            ahead = prefix(keep, before) + run
            run = ahead[:, BLOCK - 1 :] + keep[:, BLOCK - 1 :]
            weight = alpha * jnp.exp(ahead)
            colour = jnp.concatenate(got[6:9] + [jnp.zeros((5, BLOCK), F32)], axis=0)
            alpha_ref[:, cut] = alpha
            weight_ref[:, cut] = weight
            high, low = split(weight, 2)
            col_high, col_low = split(colour, 2)
            nt = (((1,), (1,)), ((), ()))
            for left, right in ((col_high, high), (col_low, high), (col_high, low)):
                render = render + lax.dot_general(left, right, nt, preferred_element_type=F32)
            kept.append((index, got, local_u, local_v, col_high, col_low))

        residual = render - jnp.concatenate([target_ref[i], jnp.zeros((5, 256), F32)], axis=0)
        res_high, res_low = split(residual, 2)
        turned = residual.T
        turn_high, turn_low = split(turned, 2)
        whole = jnp.sum((render * residual).T, axis=1, keepdims=True)
        for b in range(length // BLOCK):
            cut = slice(b * BLOCK, (b + 1) * BLOCK)
            index, got, local_u, local_v, col_high, col_low = kept[b]
            alpha = alpha_ref[:, cut]
            weight = weight_ref[:, cut]
            slope = (
                jnp.dot(turn_high, col_high, preferred_element_type=F32)
                + jnp.dot(turn_low, col_high, preferred_element_type=F32)
                + jnp.dot(turn_high, col_low, preferred_element_type=F32)
            )
            moved = slope * weight
            rest = whole - prefix(moved, upto)
            whole = rest[:, BLOCK - 1 :]
            push = moved - rest * (alpha / (1.0 - alpha))
            high, low = split(push, 2)
            moment = jnp.dot(power, high, preferred_element_type=F32) + jnp.dot(
                power, low, preferred_element_type=F32
            )
            high, low = split(weight, 2)
            hue = (
                jnp.dot(res_high, high, preferred_element_type=F32)
                + jnp.dot(res_low, high, preferred_element_type=F32)
                + jnp.dot(res_high, low, preferred_element_type=F32)
            )
            m_0, m_x, m_y, m_xx, m_xy, m_yy = [moment[k : k + 1] for k in range(6)]
            s_x = local_u * m_0 - m_x
            s_y = local_v * m_0 - m_y
            s_xx = local_u * (local_u * m_0 - 2.0 * m_x) + m_xx
            s_yy = local_v * (local_v * m_0 - 2.0 * m_y) + m_yy
            s_xy = local_u * s_y - local_v * m_x + m_xy
            back = jnp.concatenate(
                [
                    -(got[2] * s_x + got[3] * s_y),
                    -(got[4] * s_y + got[3] * s_x),
                    -0.5 * s_xx,
                    -s_xy,
                    -0.5 * s_yy,
                    m_0 / got[5],
                    hue[0:3],
                ],
                axis=0,
            )
            total_ref[...] += scatter_columns(back, index, groups)
        return carry

    lax.fori_loop(0, tiles, tile, 0)


def update_kernel(
    sizes,
    params_ref,
    m_ref,
    v_ref,
    cam_ref,
    total_ref,
    new_params_ref,
    new_m_ref,
    new_v_ref,
    view_ref,
    attr_ref,
):
    groups, focal_len, center_y = sizes
    step = pl.program_id(0)

    @pl.when(step == 0)
    def _():
        for k, value in enumerate(view_of(cam_ref)):
            view_ref[k] = value

    for q in range(8):
        attr_ref[pl.ds(q, ATTRS, stride=8), :] = params_ref[:, q * LANES : (q + 1) * LANES]
    view = [view_ref[k] for k in range(15)]
    attr = [attr_ref[8 * k : 8 * k + 8, :] for k in range(ATTRS)]
    slopes = [
        total_ref[pl.ds(pl.multiple_of(r * groups + step * 8, 8), 8), :] for r in range(SCREEN)
    ]
    _, pull = jax.vjp(lambda a: project(a, view, focal_len, center_y), attr)
    (grads,) = pull(slopes)
    for k in range(ATTRS):
        attr_ref[8 * k : 8 * k + 8, :] = grads[k]

    row = lax.broadcasted_iota(jnp.int32, (ATTRS, LANES), 0)
    rate = jnp.full((ATTRS, LANES), 0.000125, F32)
    for end, value in ((14, 0.0025), (11, 0.025), (10, 0.001), (6, 0.005), (3, 0.00016)):
        rate = jnp.where(row < end, value, rate)
    rate = rate * (1.0 / (1.0 - BETA_ONE**ADAM_STEP))
    fix_two = 1.0 / (1.0 - BETA_TWO**ADAM_STEP)
    for q in range(8):
        cut = slice(q * LANES, (q + 1) * LANES)
        grad = attr_ref[pl.ds(q, ATTRS, stride=8), :]
        first = BETA_ONE * m_ref[:, cut] + (1.0 - BETA_ONE) * grad
        second = BETA_TWO * v_ref[:, cut] + (1.0 - BETA_TWO) * grad * grad
        new_m_ref[:, cut] = first
        new_v_ref[:, cut] = second
        new_params_ref[:, cut] = params_ref[:, cut] - rate * first / (
            jnp.sqrt(second * fix_two) + ADAM_EPSILON
        )


def body(params, adam_m, adam_v, camera, target, tile_ids, tile_blocks, tile_lists, send_rows):
    spaces, capacity = send_rows.shape[1:]
    tiles, length = tile_lists.shape
    count = params.shape[1]
    tiles_all = tiles * spaces
    focal_len, center_y = max(256, tiles_all) * 5.0 / 3.0, tiles_all * 0.5
    groups = count // LANES
    heard = spaces * capacity // LANES
    rows = send_rows[0]
    steps = count // CHUNK
    vmem = pl.BlockSpec(memory_space=pltpu.VMEM)
    smem = pl.BlockSpec(memory_space=pltpu.SMEM)
    chunk = pl.BlockSpec((ATTRS, CHUNK), lambda i: (0, i))
    limits = pltpu.CompilerParams(vmem_limit_bytes=VMEM_LIMIT)
    view_sizes = (groups, focal_len, center_y)
    move_sizes = (spaces, capacity, groups)
    view_scratch = [pltpu.VMEM((15, 8, LANES), F32), pltpu.VMEM((8 * ATTRS, LANES), F32)]
    move_scratch = [
        pltpu.VMEM((spaces, SCREEN, capacity), F32),
        pltpu.VMEM((spaces, SCREEN, capacity), F32),
        pltpu.SemaphoreType.DMA((spaces,)),
        pltpu.SemaphoreType.DMA((spaces,)),
    ]

    def moving(number):
        return pltpu.CompilerParams(
            vmem_limit_bytes=VMEM_LIMIT, collective_id=number, has_side_effects=True
        )

    owned = jax.ShapeDtypeStruct((SCREEN * groups, LANES), F32)
    listed = jax.ShapeDtypeStruct((SCREEN * heard, LANES), F32)
    screen = pl.pallas_call(
        functools.partial(owner_kernel, view_sizes),
        grid=(steps,),
        in_specs=[chunk, smem],
        out_specs=vmem,
        out_shape=owned,
        scratch_shapes=view_scratch,
        compiler_params=limits,
        name="project",
    )(params, camera)
    arrived = pl.pallas_call(
        functools.partial(send_kernel, move_sizes),
        in_specs=[vmem, vmem],
        out_specs=vmem,
        out_shape=listed,
        scratch_shapes=[pltpu.VMEM((SCREEN * groups, 3 * LANES), BF16)] + move_scratch,
        compiler_params=moving(0),
        name="pick_and_send",
    )(screen, rows)
    slopes = pl.pallas_call(
        functools.partial(render_kernel, (heard, tiles, length)),
        in_specs=[vmem, vmem, vmem, smem, smem],
        out_specs=vmem,
        out_shape=listed,
        scratch_shapes=[
            pltpu.VMEM((SCREEN * heard, 3 * LANES), BF16),
            pltpu.VMEM((256, length), F32),
            pltpu.VMEM((256, length), F32),
        ],
        compiler_params=limits,
        name="render_and_back",
    )(arrived, tile_lists, target, tile_ids, tile_blocks)
    total = pl.pallas_call(
        functools.partial(return_kernel, move_sizes),
        in_specs=[vmem, vmem],
        out_specs=vmem,
        out_shape=owned,
        scratch_shapes=move_scratch,
        compiler_params=moving(1),
        name="return_and_add",
    )(slopes, rows)
    whole = jax.ShapeDtypeStruct(params.shape, F32)
    return pl.pallas_call(
        functools.partial(update_kernel, view_sizes),
        grid=(steps,),
        in_specs=[chunk, chunk, chunk, smem, vmem],
        out_specs=[chunk, chunk, chunk],
        out_shape=[whole, whole, whole],
        scratch_shapes=view_scratch,
        compiler_params=limits,
        name="gradient_and_step",
    )(params, adam_m, adam_v, camera, total)


def solution(mesh):
    wide = P(None, ("groups", "space"))
    tiles = ("groups", "space")
    return jax.shard_map(
        lambda *args: tuple(body(*args)),
        mesh=mesh,
        in_specs=(
            wide,
            wide,
            wide,
            P("groups"),
            P(tiles, None, None),
            P(tiles),
            P(tiles),
            P(tiles, None),
            P(tiles, None, None),
        ),
        out_specs=(wide, wide, wide),
        check_vma=False,
    )
```

```python
import functools

import jax
import jax.numpy as jnp
from jax import lax
from jax.experimental import pallas as pl
from jax.experimental.pallas import tpu as pltpu
from jax.sharding import PartitionSpec as P

BLOCK = 256
ADAM_STEP = 10
BETA_ONE = 0.9
BETA_TWO = 0.999
ADAM_EPSILON = 1e-15
HARM_ZERO = 0.28209479177387814
HARM_ONE = 0.4886025119029199
HARM_TWO = (
    1.0925484305920792,
    -1.0925484305920792,
    0.31539156525252005,
    -1.0925484305920792,
    0.5462742152960396,
)
HARM_THREE = (
    -0.5900435899266435,
    2.890611442640554,
    -0.4570457994644658,
    0.3731763325901154,
    -0.4570457994644658,
    1.445305721320277,
    -0.5900435899266435,
)
ATTRS = 59
SCREEN = 9
CHUNK = 1024
LANES = 128
WIDE = 256
F32 = jnp.float32
BF16 = jnp.bfloat16
VMEM_LIMIT = 56 * 1024 * 1024


def view_of(cam_ref):
    def splat(index):
        return jnp.full((8, LANES), cam_ref[index], F32)

    cos_a, sin_a = jnp.cos(splat(0)), jnp.sin(splat(0))
    cos_b, sin_b = jnp.cos(splat(1)), jnp.sin(splat(1))
    cos_c, sin_c = jnp.cos(splat(2)), jnp.sin(splat(2))
    world = [
        [
            cos_c * cos_b,
            cos_c * sin_b * sin_a - sin_c * cos_a,
            cos_c * sin_b * cos_a + sin_c * sin_a,
        ],
        [
            sin_c * cos_b,
            sin_c * sin_b * sin_a + cos_c * cos_a,
            sin_c * sin_b * cos_a - cos_c * sin_a,
        ],
        [-sin_b, cos_b * sin_a, cos_b * cos_a],
    ]
    translate = [splat(3), splat(4), 5.0 + splat(5)]
    centre = [-sum(world[k][i] * translate[k] for k in range(3)) for i in range(3)]
    return [world[i][j] for i in range(3) for j in range(3)] + translate + centre


def harmonic_basis(dir_x, dir_y, dir_z):
    dir_xx, dir_yy, dir_zz = (dir_x * dir_x, dir_y * dir_y, dir_z * dir_z)
    return [
        jnp.full_like(dir_x, HARM_ZERO),
        -HARM_ONE * dir_y,
        HARM_ONE * dir_z,
        -HARM_ONE * dir_x,
        HARM_TWO[0] * dir_x * dir_y,
        HARM_TWO[1] * dir_y * dir_z,
        HARM_TWO[2] * (2.0 * dir_zz - dir_xx - dir_yy),
        HARM_TWO[3] * dir_x * dir_z,
        HARM_TWO[4] * (dir_xx - dir_yy),
        HARM_THREE[0] * dir_y * (3.0 * dir_xx - dir_yy),
        HARM_THREE[1] * dir_x * dir_y * dir_z,
        HARM_THREE[2] * dir_y * (4.0 * dir_zz - dir_xx - dir_yy),
        HARM_THREE[3] * dir_z * (2.0 * dir_zz - 3.0 * dir_xx - 3.0 * dir_yy),
        HARM_THREE[4] * dir_x * (4.0 * dir_zz - dir_xx - dir_yy),
        HARM_THREE[5] * dir_z * (dir_xx - dir_yy),
        HARM_THREE[6] * dir_x * (dir_xx - 3.0 * dir_yy),
    ]


def project(attr, view, focal_len, center_y):
    world = [view[0:3], view[3:6], view[6:9]]
    translate, centre = view[9:12], view[12:15]
    cam = [sum(world[i][k] * attr[k] for k in range(3)) + translate[i] for i in range(3)]
    inverse = 1.0 / cam[2]
    screen_u = focal_len * cam[0] * inverse + 128.0
    screen_v = focal_len * cam[1] * inverse + center_y
    scales = [jnp.exp(attr[3 + k]) for k in range(3)]
    norm = lax.rsqrt(sum(attr[6 + k] * attr[6 + k] for k in range(4)))
    q_r, q_x, q_y, q_z = [attr[6 + k] * norm for k in range(4)]
    rotor = [
        [
            1.0 - 2.0 * (q_y * q_y + q_z * q_z),
            2.0 * (q_x * q_y - q_r * q_z),
            2.0 * (q_x * q_z + q_r * q_y),
        ],
        [
            2.0 * (q_x * q_y + q_r * q_z),
            1.0 - 2.0 * (q_x * q_x + q_z * q_z),
            2.0 * (q_y * q_z - q_r * q_x),
        ],
        [
            2.0 * (q_x * q_z - q_r * q_y),
            2.0 * (q_y * q_z + q_r * q_x),
            1.0 - 2.0 * (q_x * q_x + q_y * q_y),
        ],
    ]
    near = focal_len * inverse
    far = [-near * cam[outer] * inverse for outer in range(2)]
    mapped = []
    for outer in range(2):
        through = [near * world[outer][k] + far[outer] * world[2][k] for k in range(3)]
        mapped.append(
            [sum(through[k] * rotor[k][col] for k in range(3)) * scales[col] for col in range(3)]
        )
    cov_aa = sum(mapped[0][col] * mapped[0][col] for col in range(3)) + 0.3
    cov_ab = sum(mapped[0][col] * mapped[1][col] for col in range(3))
    cov_bb = sum(mapped[1][col] * mapped[1][col] for col in range(3)) + 0.3
    over = 1.0 / (cov_aa * cov_bb - cov_ab * cov_ab)
    opacity = 1.0 / (1.0 + jnp.exp(-attr[10]))
    offset = [attr[k] - centre[k] for k in range(3)]
    length = lax.rsqrt(sum(offset[k] * offset[k] for k in range(3)))
    basis = harmonic_basis(*[offset[k] * length for k in range(3)])
    colour = [
        jnp.maximum(sum(basis[k] * attr[11 + 3 * k + c] for k in range(16)) + 0.5, 0.0)
        for c in range(3)
    ]
    return [screen_u, screen_v, cov_bb * over, -cov_ab * over, cov_aa * over, opacity] + colour


def split(value, parts):
    out = []
    for index in range(parts):
        piece = value.astype(BF16)
        out.append(piece)
        if index + 1 < parts:
            value = value - piece.astype(F32)
    return out


def low_one_hot(index):
    rows = lax.broadcasted_iota(jnp.int32, (WIDE, index.shape[1]), 0)
    return jnp.where(rows == (index & (WIDE - 1)), 1.0, 0.0).astype(BF16)


def high_match(index, groups):
    rows = lax.broadcasted_iota(jnp.int32, (groups, index.shape[1]), 0)
    return rows == (index >> 8)


def store_pieces(lines_ref, pieces_ref):
    main = lines_ref.shape[0] // 2
    groups = main // SCREEN
    for half in range(2):
        parts = split(lines_ref[pl.ds(half, main, stride=2), :], 3)
        for k in range(2):
            start = k * WIDE + half * LANES
            pieces_ref[0:main, start : start + LANES] = parts[k]
        pieces_ref[main:, half * LANES : (half + 1) * LANES] = parts[2][0 : 2 * groups]
    pieces_ref[main:, WIDE:] = jnp.zeros((2 * groups, WIDE), BF16)


def gather_columns(pieces, index, hot):
    groups = pieces.shape[0] // (SCREEN + 2)
    picked = jnp.dot(
        pieces, jnp.concatenate([hot, hot], axis=0), preferred_element_type=F32
    )
    match = high_match(index, groups)
    out = []
    for r in range(SCREEN):
        value = picked[r * groups : (r + 1) * groups]
        if r < 2:
            value = value + picked[(SCREEN + r) * groups : (SCREEN + r + 1) * groups]
        out.append(jnp.sum(jnp.where(match, value, 0.0), axis=0, keepdims=True))
    return out


def scatter_columns(rows, index, hot, groups):
    match = jnp.where(high_match(index, groups), 1.0, 0.0).astype(BF16)
    total = None
    for piece in split(rows, 2):
        left = jnp.concatenate([piece[r : r + 1] * match for r in range(SCREEN)], axis=0)
        part = lax.dot_general(
            left, hot, (((1,), (1,)), ((), ())), preferred_element_type=F32
        )
        total = part if total is None else total + part
    return total


def store_lines(lines_ref, wide):
    for half in range(2):
        lines_ref[pl.ds(half, wide.shape[0], stride=2), :] = wide[
            :, half * LANES : (half + 1) * LANES
        ]


def owner_kernel(sizes, params_ref, cam_ref, screen_ref, view_ref, attr_ref):
    groups, focal_len, center_y = sizes
    step = pl.program_id(0)

    @pl.when(step == 0)
    def _():
        for k, value in enumerate(view_of(cam_ref)):
            view_ref[k] = value

    for q in range(8):
        attr_ref[pl.ds(q, ATTRS, stride=8), :] = params_ref[:, q * LANES : (q + 1) * LANES]
    view = [view_ref[k] for k in range(15)]
    attr = [attr_ref[8 * k : 8 * k + 8, :] for k in range(ATTRS)]
    values = project(attr, view, focal_len, center_y)
    for r in range(SCREEN):
        screen_ref[pl.ds(pl.multiple_of(r * groups + step * 8, 8), 8), :] = values[r]


def greet(spaces):
    me = lax.axis_index("space")
    barrier = pltpu.get_barrier_semaphore()

    def signal(t, carry):
        pl.semaphore_signal(
            barrier,
            inc=1,
            device_id={"space": lax.rem(me + t, spaces)},
            device_id_type=pl.DeviceIdType.MESH,
        )
        return carry

    lax.fori_loop(1, spaces, signal, 0)
    pl.semaphore_wait(barrier, spaces - 1)


def packet_copy(kept_ref, land_ref, send_sem, recv_sem, source, target):
    return pltpu.make_async_remote_copy(
        src_ref=kept_ref.at[target],
        dst_ref=land_ref.at[source],
        send_sem=send_sem.at[target],
        recv_sem=recv_sem.at[source],
        device_id={"space": target},
        device_id_type=pl.DeviceIdType.MESH,
    )


def send_kernel(
    sizes, screen_ref, rows_ref, lines_ref, pieces_ref, kept_ref, land_ref, send_sem, recv_sem
):
    spaces, capacity, groups = sizes
    per = capacity // LANES
    heard = spaces * per
    me = lax.axis_index("space")
    store_pieces(screen_ref, pieces_ref)

    def pick(d):
        index = rows_ref[pl.ds(d, 1), :]
        got = gather_columns(pieces_ref[...], index, low_one_hot(index))
        return jnp.concatenate(got, axis=0)

    def unpack(s, packet):
        for r in range(SCREEN):
            for k in range(per):
                lines_ref[pl.ds(r * heard + s * per + k, 1), :] = packet[
                    r : r + 1, k * LANES : (k + 1) * LANES
                ]

    greet(spaces)

    def send(t, carry):
        d = lax.rem(me + t, spaces)
        kept_ref[d] = pick(d)
        packet_copy(kept_ref, land_ref, send_sem, recv_sem, me, d).start()
        return carry

    lax.fori_loop(1, spaces, send, 0)
    unpack(me, pick(me))

    def take(t, carry):
        s = lax.rem(me + spaces - t, spaces)
        packet_copy(kept_ref, land_ref, send_sem, recv_sem, s, s).wait_recv()
        unpack(s, land_ref[s])
        return carry

    lax.fori_loop(1, spaces, take, 0)

    def done(t, carry):
        d = lax.rem(me + t, spaces)
        packet_copy(kept_ref, land_ref, send_sem, recv_sem, me, d).wait_send()
        return carry

    lax.fori_loop(1, spaces, done, 0)


def return_kernel(
    sizes, slopes_ref, rows_ref, out_ref, total_ref, kept_ref, land_ref, send_sem, recv_sem
):
    spaces, capacity, groups = sizes
    per = capacity // LANES
    heard = spaces * per
    me = lax.axis_index("space")

    def pack(d):
        for r in range(SCREEN):
            for k in range(per):
                kept_ref[d, r : r + 1, k * LANES : (k + 1) * LANES] = slopes_ref[
                    pl.ds(r * heard + d * per + k, 1), :
                ]

    greet(spaces)

    def send(t, carry):
        d = lax.rem(me + t, spaces)
        pack(d)
        packet_copy(kept_ref, land_ref, send_sem, recv_sem, me, d).start()
        return carry

    lax.fori_loop(1, spaces, send, 0)
    pack(me)

    def spread(packet, s):
        index = rows_ref[pl.ds(s, 1), :]
        return scatter_columns(packet, index, low_one_hot(index), groups // 2)

    total_ref[...] = spread(kept_ref[me], me)

    def take(t, carry):
        s = lax.rem(me + spaces - t, spaces)
        packet_copy(kept_ref, land_ref, send_sem, recv_sem, s, s).wait_recv()
        total_ref[...] += spread(land_ref[s], s)
        return carry

    lax.fori_loop(1, spaces, take, 0)
    store_lines(out_ref, total_ref[...])

    def done(t, carry):
        d = lax.rem(me + t, spaces)
        packet_copy(kept_ref, land_ref, send_sem, recv_sem, me, d).wait_send()
        return carry

    lax.fori_loop(1, spaces, done, 0)


def render_kernel(
    sizes,
    lines_ref,
    lists_ref,
    target_ref,
    ids_ref,
    blocks_ref,
    out_ref,
    total_ref,
    pieces_ref,
    high_ref,
    low_ref,
    ratio_ref,
):
    groups, tiles, length = sizes
    store_pieces(lines_ref, pieces_ref)
    total_ref[...] = jnp.zeros_like(total_ref)

    earlier = lax.broadcasted_iota(jnp.int32, (BLOCK, BLOCK), 0)
    later = lax.broadcasted_iota(jnp.int32, (BLOCK, BLOCK), 1)
    before = jnp.where(earlier < later, 1.0, 0.0).astype(BF16)
    before = jnp.concatenate([before, before], axis=0)
    upto = jnp.where(earlier <= later, 1.0, 0.0).astype(BF16)
    upto = jnp.concatenate([upto, upto], axis=0)
    pixel = lax.broadcasted_iota(jnp.int32, (8, 256), 1)
    which = lax.broadcasted_iota(jnp.int32, (8, 256), 0)
    local_x = (pixel % 16 - 8).astype(F32)
    local_y = (pixel // 16 - 8).astype(F32)
    power = jnp.where(which == 0, 1.0, 0.0)
    for row, term in enumerate(
        [local_x, local_y, local_x * local_x, local_x * local_y, local_y * local_y]
    ):
        power = jnp.where(which == row + 1, term, power)
    power = power.astype(BF16)
    offsets = (lax.broadcasted_iota(jnp.int32, (16, BLOCK), 0) - 8).astype(F32)

    def prefix(value, ones):
        return jnp.dot(
            jnp.concatenate(split(value, 2), axis=1), ones, preferred_element_type=F32
        )

    def both(high, low):
        return jnp.concatenate([high.astype(F32), low.astype(F32)], axis=0).astype(BF16)

    def front(i, slot):
        tile_id = ids_ref[i]
        live = blocks_ref[i] * BLOCK
        index_row = lists_ref[pl.ds(i, 1), :]
        base_x = ((tile_id % 16) * 16 + 8).astype(F32)
        base_y = ((tile_id // 16) * 16 + 8).astype(F32)
        kept = []
        run = jnp.zeros((256, 1), F32)
        render = jnp.zeros((8, 256), F32)
        for b in range(length // BLOCK):
            index = index_row[:, b * BLOCK : (b + 1) * BLOCK]
            cut = slice(slot * length + b * BLOCK, slot * length + (b + 1) * BLOCK)
            hot = low_one_hot(index)
            got = gather_columns(pieces_ref[...], index, hot)
            spot = lax.broadcasted_iota(jnp.int32, (1, BLOCK), 1) + b * BLOCK
            shown = jnp.where(spot < live, got[5], 0.0)
            local_u = got[0] - base_x
            local_v = got[1] - base_y
            delta_x = local_u - offsets
            delta_y = local_v - offsets
            part_x = -0.5 * got[2] * delta_x * delta_x
            part_y = -0.5 * got[4] * delta_y * delta_y
            cross = -got[3] * delta_y
            alpha = jnp.concatenate(
                [
                    shown
                    * jnp.exp(
                        part_x + part_y[y : y + 1, :] + delta_x * cross[y : y + 1, :]
                    )
                    for y in range(16)
                ],
                axis=0,
            )
            keep = jnp.log(1.0 - alpha)
            ahead = prefix(keep, before) + run
            run = ahead[:, BLOCK - 1 :] + keep[:, BLOCK - 1 :]
            weight = alpha * jnp.exp(ahead)
            colour = jnp.concatenate(got[6:9] + [jnp.zeros((5, BLOCK), F32)], axis=0)
            over = pl.reciprocal(1.0 - alpha, approx=True)
            over = over * (2.0 - (1.0 - alpha) * over)
            ratio_ref[:, cut] = alpha * over
            high, low = split(weight, 2)
            high_ref[:, cut] = high
            low_ref[:, cut] = low
            col_high, col_low = split(colour, 2)
            nt = (((1,), (1,)), ((), ()))
            stacked = both(col_high, col_low)
            part = lax.dot_general(stacked, high, nt, preferred_element_type=F32)
            render = render + part[0:8] + part[8:16]
            render = render + lax.dot_general(col_high, low, nt, preferred_element_type=F32)
            kept.append((index, hot, got, local_u, local_v))
        return render, kept

    def rear(i, slot, render, kept):
        residual = render - jnp.concatenate([target_ref[i], jnp.zeros((5, 256), F32)], axis=0)
        res_high, res_low = split(residual, 2)
        res_both = both(res_high, res_low)
        whole = jnp.sum(render * residual, axis=0, keepdims=True)
        turned = jnp.concatenate([residual[0:3], whole, residual[4:8]], axis=0).T
        red, green, blue, whole = [turned[:, k : k + 1] for k in range(4)]
        for b in range(length // BLOCK):
            cut = slice(slot * length + b * BLOCK, slot * length + (b + 1) * BLOCK)
            index, hot, got, local_u, local_v = kept[b]
            weight_high = high_ref[:, cut]
            weight_low = low_ref[:, cut]
            weight = weight_high.astype(F32) + weight_low.astype(F32)
            slope = red * got[6] + green * got[7] + blue * got[8]
            moved = slope * weight
            rest = whole - prefix(moved, upto)
            whole = rest[:, BLOCK - 1 :]
            push = moved - rest * ratio_ref[:, cut]
            high, low = split(push, 2)
            moment = jnp.dot(power, high, preferred_element_type=F32) + jnp.dot(
                power, low, preferred_element_type=F32
            )
            part = jnp.dot(res_both, weight_high, preferred_element_type=F32)
            hue = part[0:8] + part[8:16]
            hue = hue + jnp.dot(res_high, weight_low, preferred_element_type=F32)
            m_0, m_x, m_y, m_xx, m_xy, m_yy = [moment[k : k + 1] for k in range(6)]
            s_x = local_u * m_0 - m_x
            s_y = local_v * m_0 - m_y
            s_xx = local_u * (local_u * m_0 - 2.0 * m_x) + m_xx
            s_yy = local_v * (local_v * m_0 - 2.0 * m_y) + m_yy
            s_xy = local_u * s_y - local_v * m_x + m_xy
            back = jnp.concatenate(
                [
                    -(got[2] * s_x + got[3] * s_y),
                    -(got[4] * s_y + got[3] * s_x),
                    -0.5 * s_xx,
                    -s_xy,
                    -0.5 * s_yy,
                    m_0 / got[5],
                    hue[0:3],
                ],
                axis=0,
            )
            total_ref[...] += scatter_columns(back, index, hot, groups // 2)

    together = 2 - tiles % 2

    def some_tiles(i, carry):
        states = [front(together * i + slot, slot) for slot in range(together)]
        for slot in range(together):
            rear(together * i + slot, slot, *states[slot])
        return carry

    lax.fori_loop(0, tiles // together, some_tiles, 0)
    store_lines(out_ref, total_ref[...])


def update_kernel(
    sizes,
    params_ref,
    m_ref,
    v_ref,
    cam_ref,
    total_ref,
    new_params_ref,
    new_m_ref,
    new_v_ref,
    view_ref,
    attr_ref,
):
    groups, focal_len, center_y = sizes
    step = pl.program_id(0)

    @pl.when(step == 0)
    def _():
        for k, value in enumerate(view_of(cam_ref)):
            view_ref[k] = value

    for q in range(8):
        attr_ref[pl.ds(q, ATTRS, stride=8), :] = params_ref[:, q * LANES : (q + 1) * LANES]
    view = [view_ref[k] for k in range(15)]
    attr = [attr_ref[8 * k : 8 * k + 8, :] for k in range(ATTRS)]
    slopes = [
        total_ref[pl.ds(pl.multiple_of(r * groups + step * 8, 8), 8), :] for r in range(SCREEN)
    ]
    _, pull = jax.vjp(lambda a: project(a, view, focal_len, center_y), attr)
    (grads,) = pull(slopes)
    for k in range(ATTRS):
        attr_ref[8 * k : 8 * k + 8, :] = grads[k]

    row = lax.broadcasted_iota(jnp.int32, (ATTRS, LANES), 0)
    rate = jnp.full((ATTRS, LANES), 0.000125, F32)
    for end, value in ((14, 0.0025), (11, 0.025), (10, 0.001), (6, 0.005), (3, 0.00016)):
        rate = jnp.where(row < end, value, rate)
    rate = rate * (1.0 / (1.0 - BETA_ONE**ADAM_STEP))
    fix_two = 1.0 / (1.0 - BETA_TWO**ADAM_STEP)
    for q in range(8):
        cut = slice(q * LANES, (q + 1) * LANES)
        grad = attr_ref[pl.ds(q, ATTRS, stride=8), :]
        first = BETA_ONE * m_ref[:, cut] + (1.0 - BETA_ONE) * grad
        second = BETA_TWO * v_ref[:, cut] + (1.0 - BETA_TWO) * grad * grad
        new_m_ref[:, cut] = first
        new_v_ref[:, cut] = second
        new_params_ref[:, cut] = params_ref[:, cut] - rate * first / (
            jnp.sqrt(second * fix_two) + ADAM_EPSILON
        )


def render_scratch(heard, length):
    return [
        pltpu.VMEM((SCREEN * heard // 2, WIDE), F32),
        pltpu.VMEM(((SCREEN + 2) * heard // 2, 2 * WIDE), BF16),
        pltpu.VMEM((256, 2 * length), BF16),
        pltpu.VMEM((256, 2 * length), BF16),
        pltpu.VMEM((256, 2 * length), F32),
    ]


def body(params, adam_m, adam_v, camera, target, tile_ids, tile_blocks, tile_lists, send_rows):
    spaces, capacity = send_rows.shape[1:]
    tiles, length = tile_lists.shape
    count = params.shape[1]
    tiles_all = tiles * spaces
    focal_len, center_y = max(256, tiles_all) * 5.0 / 3.0, tiles_all * 0.5
    groups = count // LANES
    heard = spaces * capacity // LANES
    rows = send_rows[0]
    steps = count // CHUNK
    vmem = pl.BlockSpec(memory_space=pltpu.VMEM)
    smem = pl.BlockSpec(memory_space=pltpu.SMEM)
    chunk = pl.BlockSpec((ATTRS, CHUNK), lambda i: (0, i))
    limits = pltpu.CompilerParams(vmem_limit_bytes=VMEM_LIMIT)
    view_sizes = (groups, focal_len, center_y)
    move_sizes = (spaces, capacity, groups)
    view_scratch = [pltpu.VMEM((15, 8, LANES), F32), pltpu.VMEM((8 * ATTRS, LANES), F32)]
    move_scratch = [
        pltpu.VMEM((spaces, SCREEN, capacity), F32),
        pltpu.VMEM((spaces, SCREEN, capacity), F32),
        pltpu.SemaphoreType.DMA((spaces,)),
        pltpu.SemaphoreType.DMA((spaces,)),
    ]

    def moving(number):
        return pltpu.CompilerParams(
            vmem_limit_bytes=VMEM_LIMIT, collective_id=number, has_side_effects=True
        )

    owned = jax.ShapeDtypeStruct((SCREEN * groups, LANES), F32)
    listed = jax.ShapeDtypeStruct((SCREEN * heard, LANES), F32)
    screen = pl.pallas_call(
        functools.partial(owner_kernel, view_sizes),
        grid=(steps,),
        in_specs=[chunk, smem],
        out_specs=vmem,
        out_shape=owned,
        scratch_shapes=view_scratch,
        compiler_params=limits,
        name="project",
    )(params, camera)
    arrived = pl.pallas_call(
        functools.partial(send_kernel, move_sizes),
        in_specs=[vmem, vmem],
        out_specs=vmem,
        out_shape=listed,
        scratch_shapes=[pltpu.VMEM(((SCREEN + 2) * groups // 2, 2 * WIDE), BF16)] + move_scratch,
        compiler_params=moving(0),
        name="pick_and_send",
    )(screen, rows)
    slopes = pl.pallas_call(
        functools.partial(render_kernel, (heard, tiles, length)),
        in_specs=[vmem, vmem, vmem, smem, smem],
        out_specs=vmem,
        out_shape=listed,
        scratch_shapes=render_scratch(heard, length),
        compiler_params=limits,
        name="render_and_back",
    )(arrived, tile_lists, target, tile_ids, tile_blocks)
    total = pl.pallas_call(
        functools.partial(return_kernel, move_sizes),
        in_specs=[vmem, vmem],
        out_specs=vmem,
        out_shape=owned,
        scratch_shapes=[pltpu.VMEM((SCREEN * groups // 2, WIDE), F32)] + move_scratch,
        compiler_params=moving(1),
        name="return_and_add",
    )(slopes, rows)
    whole = jax.ShapeDtypeStruct(params.shape, F32)
    return pl.pallas_call(
        functools.partial(update_kernel, view_sizes),
        grid=(steps,),
        in_specs=[chunk, chunk, chunk, smem, vmem],
        out_specs=[chunk, chunk, chunk],
        out_shape=[whole, whole, whole],
        scratch_shapes=view_scratch,
        compiler_params=limits,
        name="gradient_and_step",
    )(params, adam_m, adam_v, camera, total)


def solution(mesh):
    wide = P(None, ("groups", "space"))
    tiles = ("groups", "space")
    return jax.shard_map(
        lambda *args: tuple(body(*args)),
        mesh=mesh,
        in_specs=(
            wide,
            wide,
            wide,
            P("groups"),
            P(tiles, None, None),
            P(tiles),
            P(tiles),
            P(tiles, None),
            P(tiles, None, None),
        ),
        out_specs=(wide, wide, wide),
        check_vma=False,
    )
```
